1024 devices in a mesh: outer: 8 (over y_hi, core), inner: 128 (over z, y_lo, x).
Axes of the slice: x: 8, y: 8 (y_hi: 4, y_lo: 2; y = y_hi * 2 + y_lo), z: 8, core: 2. Of those that a mesh axis runs over, the one named last changes fastest.
Arguments:
- tok_mant: bfloat16 [256, 16384], P('inner', 'outer'), may hold values from -6 to 6
- tok_expo: int32 [256, 512], P('inner', 'outer'), may hold values from -3 to 1
- gate_mant: bfloat16 [16384, 53248], P('outer', 'inner'), may hold values from -0.046875 to 0.046875
- gate_expo: int32 [512, 53248], P('outer', 'inner'), may hold values from -3 to 1
- up_mant: bfloat16 [16384, 53248], P('outer', 'inner'), may hold values from -0.046875 to 0.046875
- up_expo: int32 [512, 53248], P('outer', 'inner'), may hold values from -3 to 1
Outputs:
- hidden: bfloat16 [256, 53248], P('outer', 'inner')
The draws below stay inside these ranges and needn't reach their ends.
All inputs are finite; a program needn't handle non-finite values.
Results may differ from the reference program's by a relative error of at most 0.0017.
Values may be sent and summed in bfloat16 or wider, within the bound.
No kernel may reach another device: no remote copies, remote signals or barrier semaphores. Data moves between devices by JAX's collectives and lax.ppermute only.
A program may use at most 32 MiB of HBM per device.

```python
import math
import jax
import jax.numpy as jnp
from jax import lax

K = 16384
FF = 53248
BLOCK = 32
TOKENS = 256
KB = 512


def touch_ends(values, own_key, least, top_value):
    place = [jax.random.randint(jax.random.fold_in(own_key, axis), (), 0, length) for axis, length in enumerate(values.shape)]
    main_axis = values.shape.index(max(values.shape))
    neighbour = place[:main_axis] + [(place[main_axis] + 1) % values.shape[main_axis]] + place[main_axis + 1:]
    return values.at[tuple(place)].set(least).at[tuple(neighbour)].set(top_value)


def level_of(rng, extent, cuts, low, high):
    loudness, own = 1.0, jax.random.fold_in(rng, 6)
    for dim, shards_of in cuts:
        draws = jnp.exp(jax.random.uniform(jax.random.fold_in(own, dim), (shards_of,), jnp.float32, low / len(cuts), high / len(cuts)))
        loudness = loudness * jnp.repeat(draws, extent[dim] // shards_of).reshape([-1 if axis == dim else 1 for axis in range(len(extent))])
    return loudness


def centred(stream_key, extent, scale, most, split=(), held_as=jnp.bfloat16):
    loudness = level_of(stream_key, extent, split, -0.22, 0.18) if split else 1.0
    entries = jax.random.normal(stream_key, extent, jnp.float32) * scale * loudness
    return jnp.minimum(jnp.maximum(entries, -most), most).astype(held_as)


def setup_inputs(seed: int = 0) -> dict:
    arg_keys = jax.random.split(jax.random.key(seed), 7)
    return {
        "tok_mant": centred(arg_keys[0], (TOKENS, K), 1.0, 6.0, ((0, 128), (1, 8))),
        "tok_expo": touch_ends(jax.random.randint(arg_keys[1], (TOKENS, KB), -3, 2), jax.random.fold_in(arg_keys[1], 1), -3, 1).astype(jnp.int32),
        "gate_mant": centred(arg_keys[2], (K, FF), K ** -0.5, 0.046875, ((0, 8), (1, 128))),
        "gate_expo": touch_ends(jax.random.randint(arg_keys[3], (KB, FF), -3, 2), jax.random.fold_in(arg_keys[3], 1), -3, 1).astype(jnp.int32),
        "up_mant": centred(arg_keys[4], (K, FF), K ** -0.5, 0.046875, ((0, 8), (1, 128))),
        "up_expo": touch_ends(jax.random.randint(arg_keys[5], (KB, FF), -3, 2), jax.random.fold_in(arg_keys[5], 1), -3, 1).astype(jnp.int32),
    }


def reference(tok_mant, tok_expo, gate_mant, gate_expo, up_mant, up_expo):
    rows = tok_mant.shape[0]
    scale = jnp.exp2(tok_expo.astype(jnp.float32))
    tokens = (tok_mant.astype(jnp.float32).reshape(rows, KB, BLOCK) * scale[:, :, None]).reshape(rows, K).astype(jnp.bfloat16)
    width = math.gcd(FF, 1024)
    count = FF // width

    def column_block(index):
        start = (index * width).astype(jnp.int32)
        outs = []
        for mant, expo in ((gate_mant, gate_expo), (up_mant, up_expo)):
            piece = lax.dynamic_slice_in_dim(mant, start, width, 1).astype(jnp.float32)
            piece_expo = lax.dynamic_slice_in_dim(expo, start, width, 1)
            weight = (piece.reshape(KB, BLOCK, width) * jnp.exp2(piece_expo.astype(jnp.float32))[:, None, :]).reshape(K, width).astype(jnp.bfloat16)
            outs.append(jnp.dot(tokens, weight, preferred_element_type=jnp.float32))
        return (jax.nn.silu(outs[0]) * outs[1]).astype(jnp.bfloat16)

    blocks = lax.map(column_block, jnp.arange(count, dtype=jnp.int32))
    return jnp.transpose(blocks, (1, 0, 2)).reshape(rows, FF)
```

```python
import jax
import jax.numpy as jnp
from jax import lax
from jax.sharding import Mesh
from jax.sharding import PartitionSpec as P

AXES = ("yh", "c", "z", "yl", "x")
SIZES = (4, 2, 8, 2, 8)
OUTER = ("yh", "c")
INNER = ("z", "yl", "x")


def scaled_rows(mant, expo):
    rows, width = mant.shape
    factor = jnp.exp2(expo.astype(jnp.float32))
    return (
        (mant.astype(jnp.float32).reshape(rows, width // 32, 32) * factor[:, :, None])
        .reshape(rows, width)
        .astype(jnp.bfloat16)
    )


def scaled_columns(mant, expo):
    depth, width = mant.shape
    factor = jnp.exp2(expo.astype(jnp.float32))
    return (
        (mant.astype(jnp.float32).reshape(depth // 32, 32, width) * factor[:, None, :])
        .reshape(depth, width)
        .astype(jnp.bfloat16)
    )


def gathered(block, axes, count):
    copies = jnp.broadcast_to(block[None], (count,) + block.shape)
    return lax.all_to_all(copies, axes, 0, 0)


def summed_shares(terms):
    width = terms.shape[1]
    parts = terms.reshape(4, 2, 32, width)
    core, row = lax.axis_index("c"), lax.axis_index("yh")
    own = lax.dynamic_index_in_dim(parts, core, 1, False)
    other = lax.dynamic_index_in_dim(parts, 1 - core, 1, False)
    pair = own + lax.ppermute(other, "c", [(0, 1), (1, 0)])
    total = lax.dynamic_index_in_dim(pair, row, 0, False)
    for step in (2, 1, 3):
        ahead = lax.dynamic_index_in_dim(pair, (row + step) % 4, 0, False)
        total = total + lax.ppermute(ahead, "yh", [(i, (i + step) % 4) for i in range(4)])
    return total


def local(tok_mant, tok_expo, gate_mant, gate_expo, up_mant, up_expo):
    tokens = scaled_rows(tok_mant, tok_expo)
    weights = jnp.concatenate(
        (scaled_columns(gate_mant, gate_expo), scaled_columns(up_mant, up_expo)), axis=1
    )
    half = gate_mant.shape[1]
    everyone = gathered(tokens, INNER, 128).reshape(256, tokens.shape[1])
    terms = jnp.dot(everyone, weights, preferred_element_type=jnp.float32)
    summed = summed_shares(terms)
    return (jax.nn.silu(summed[:, :half]) * summed[:, half:]).astype(jnp.bfloat16)


def solution(mesh):
    fine = Mesh(mesh.devices.reshape(SIZES), AXES)
    placed = (
        P(INNER, OUTER),
        P(INNER, OUTER),
        P(OUTER, INNER),
        P(OUTER, INNER),
        P(OUTER, INNER),
        P(OUTER, INNER),
    )
    return jax.shard_map(
        local, mesh=fine, in_specs=placed, out_specs=P(OUTER, INNER), check_vma=False
    )
```

```python
import jax
import jax.numpy as jnp
from jax import lax
from jax.experimental import pallas as pl
from jax.experimental.pallas import tpu as pltpu
from jax.sharding import Mesh
from jax.sharding import PartitionSpec as P

AXES = ("yh", "c", "zh", "zl", "yl", "xh", "xl")
SIZES = (4, 2, 4, 2, 2, 4, 2)
OUTER = ("yh", "c")
INNER = ("zh", "zl", "yl", "xh", "xl")
FAR = ("zh", "xh")
NEAR = ("zl", "yl", "xl")


def copies_kernel(mant_ref, expo_ref, out_ref):
    blocks, width = expo_ref.shape[1], mant_ref.shape[1]
    group = lax.broadcasted_iota(jnp.int32, (blocks, width), 1) // (width // blocks)
    spread = (group == lax.broadcasted_iota(jnp.int32, (blocks, width), 0)).astype(jnp.bfloat16)
    factor = jnp.exp2(expo_ref[...].astype(jnp.float32)).astype(jnp.bfloat16)
    scale = jnp.dot(factor, spread, preferred_element_type=jnp.float32)
    scaled = (mant_ref[...].astype(jnp.float32) * scale).astype(jnp.bfloat16)
    out_ref[...] = jnp.broadcast_to(scaled[None], out_ref.shape)


def scaled_copies(mant, expo, count):
    return pl.pallas_call(
        copies_kernel,
        out_shape=jax.ShapeDtypeStruct((count,) + mant.shape, jnp.bfloat16),
        compiler_params=pltpu.CompilerParams(vmem_limit_bytes=56 << 20),
    )(mant, expo)


def weights_kernel(gate_ref, gate_expo_ref, up_ref, up_expo_ref, out_ref):
    def scaled(mant_ref, expo_ref):
        factor = jnp.exp2(expo_ref[...].astype(jnp.float32)).astype(jnp.bfloat16)
        scale = lax.dot_general(
            factor, spread, (((0,), (0,)), ((), ())), preferred_element_type=jnp.float32
        )
        return (mant_ref[...].astype(jnp.float32) * scale).astype(jnp.bfloat16)

    blocks, half, width = gate_expo_ref.shape[0], gate_ref.shape[0], gate_ref.shape[1]
    first = pl.program_id(0) * width
    block = (first + lax.broadcasted_iota(jnp.int32, (blocks, width), 1)) // 32
    spread = (block == lax.broadcasted_iota(jnp.int32, (blocks, width), 0)).astype(jnp.bfloat16)
    out_ref[:half] = scaled(gate_ref, gate_expo_ref)
    out_ref[half:] = scaled(up_ref, up_expo_ref)


def scaled_weights(gate_mant, gate_expo, up_mant, up_expo):
    depth, half = gate_mant.shape
    steps = 4
    mant = pl.BlockSpec((half, depth // steps), lambda i: (0, i))
    expo = pl.BlockSpec(gate_expo.shape, lambda i: (0, 0))
    return pl.pallas_call(
        weights_kernel,
        grid=(steps,),
        in_specs=[mant, expo, mant, expo],
        out_specs=pl.BlockSpec((2 * half, depth // steps), lambda i: (0, i)),
        out_shape=jax.ShapeDtypeStruct((2 * half, depth), jnp.bfloat16),
        compiler_params=pltpu.CompilerParams(vmem_limit_bytes=24 << 20),
        cost_estimate=pl.CostEstimate(
            flops=4 * half * depth * 64, bytes_accessed=8 * half * depth, transcendentals=0
        ),
    )(gate_mant.T, gate_expo, up_mant.T, up_expo)


def product_kernel(side_ref, rows_ref, weights_ref, out_ref):
    width = rows_ref.shape[-1]
    rows = jnp.transpose(rows_ref[0], (2, 0, 3, 1, 4, 5)).reshape(-1, width)
    out_ref[...] = lax.dot_general(
        rows, weights_ref[...], (((1,), (1,)), ((), ())), preferred_element_type=jnp.float32
    )


def product(side, everyone, weights):
    count, units = everyone.size // everyone.shape[-1] // 2, weights.shape[0]
    return pl.pallas_call(
        product_kernel,
        grid_spec=pltpu.PrefetchScalarGridSpec(
            num_scalar_prefetch=1,
            grid=(1,),
            in_specs=[
                pl.BlockSpec((1,) + everyone.shape[1:], lambda i, side: (side[0],) + (0,) * 6),
                pl.BlockSpec(weights.shape, lambda i, side: (0, 0)),
            ],
            out_specs=pl.BlockSpec((count, units), lambda i, side: (0, 0)),
        ),
        out_shape=jax.ShapeDtypeStruct((count, units), jnp.float32),
        compiler_params=pltpu.CompilerParams(vmem_limit_bytes=24 << 20),
        cost_estimate=pl.CostEstimate(
            flops=2 * count * weights.size, bytes_accessed=2 * weights.size, transcendentals=0
        ),
    )(side.reshape(1), everyone, weights)


def summed_shares(everyone, weights):
    core = lax.axis_index("c")
    theirs = lax.ppermute(product(1 - core, everyone, weights), "c", [(0, 1), (1, 0)])
    pair = product(core, everyone, weights) + theirs
    parts = lax.all_to_all(pair.reshape(4, 32, -1), "yh", 0, 0)
    return jnp.sum(parts, axis=0)


def gathered(tok_mant, tok_expo):
    far = lax.all_to_all(scaled_copies(tok_mant, tok_expo, 16), FAR, 0, 0)
    near = lax.all_to_all(jnp.broadcast_to(far[None], (8,) + far.shape), NEAR, 0, 0)
    return near.reshape((2, 2, 2, 4, 4) + tok_mant.shape)


def local(tok_mant, tok_expo, gate_mant, gate_expo, up_mant, up_expo):
    weights = scaled_weights(gate_mant, gate_expo, up_mant, up_expo)
    half = gate_mant.shape[1]
    everyone = gathered(tok_mant, tok_expo)
    summed = summed_shares(everyone, weights)
    return (jax.nn.silu(summed[:, :half]) * summed[:, half:]).astype(jnp.bfloat16)


def solution(mesh):
    fine = Mesh(mesh.devices.reshape(SIZES), AXES)
    placed = (
        P(INNER, OUTER),
        P(INNER, OUTER),
        P(OUTER, INNER),
        P(OUTER, INNER),
        P(OUTER, INNER),
        P(OUTER, INNER),
    )
    return jax.shard_map(
        local, mesh=fine, in_specs=placed, out_specs=P(OUTER, INNER), check_vma=False
    )
```

```python
import itertools

import jax
import jax.numpy as jnp
from jax import lax
from jax.experimental import pallas as pl
from jax.experimental.pallas import tpu as pltpu
from jax.sharding import Mesh
from jax.sharding import PartitionSpec as P

AXES = ("yh", "c", "zh", "zl", "yl", "xh", "xl")
SIZES = (4, 2, 4, 2, 2, 4, 2)
OUTER = ("yh", "c")
INNER = ("zh", "zl", "yl", "xh", "xl")
FAR = ("zh", "yl", "xh")


def copies_kernel(mant_ref, expo_ref, out_ref):
    blocks, width = expo_ref.shape[1], mant_ref.shape[1]
    group = lax.broadcasted_iota(jnp.int32, (blocks, width), 1) // (width // blocks)
    spread = (group == lax.broadcasted_iota(jnp.int32, (blocks, width), 0)).astype(jnp.bfloat16)
    factor = jnp.exp2(expo_ref[...].astype(jnp.float32)).astype(jnp.bfloat16)
    scale = jnp.dot(factor, spread, preferred_element_type=jnp.float32)
    scaled = (mant_ref[...].astype(jnp.float32) * scale).astype(jnp.bfloat16)
    out_ref[...] = jnp.broadcast_to(scaled[None], out_ref.shape)


def scaled_copies(mant, expo, count):
    return pl.pallas_call(
        copies_kernel,
        out_shape=jax.ShapeDtypeStruct((count,) + mant.shape, jnp.bfloat16),
        compiler_params=pltpu.CompilerParams(vmem_limit_bytes=56 << 20),
    )(mant, expo)


def weights_kernel(gate_ref, gate_expo_ref, up_ref, up_expo_ref, wide_ref, rest_ref):
    def scaled(mant_ref, expo_ref):
        factor = jnp.exp2(expo_ref[...].astype(jnp.float32)).astype(jnp.bfloat16)
        scale = lax.dot_general(
            factor, spread, (((0,), (0,)), ((), ())), preferred_element_type=jnp.float32
        )
        return (mant_ref[...].astype(jnp.float32) * scale).astype(jnp.bfloat16)

    blocks, width = gate_expo_ref.shape[0], gate_ref.shape[1]
    step = pl.program_id(0)
    block = (step * width + lax.broadcasted_iota(jnp.int32, (blocks, width), 1)) // 32
    spread = (block == lax.broadcasted_iota(jnp.int32, (blocks, width), 0)).astype(jnp.bfloat16)
    both = (scaled(gate_ref, gate_expo_ref), scaled(up_ref, up_expo_ref))
    turned = jnp.concatenate(both, axis=0).T
    wide = wide_ref.shape[1]
    rest = turned.shape[1] - wide
    wide_ref[...] = turned[:, :wide]
    for half in range(2):

        @pl.when(step == half)
        def _():
            rest_ref[:, half * rest : (half + 1) * rest] = turned[:, wide:]


def scaled_weights(gate_mant, gate_expo, up_mant, up_expo):
    depth, half = gate_mant.shape
    width = depth // 2
    wide = 2 * half // 128 * 128
    rest = 2 * half - wide
    mant = pl.BlockSpec((half, width), lambda i: (0, i))
    expo = pl.BlockSpec(gate_expo.shape, lambda i: (0, 0))
    return pl.pallas_call(
        weights_kernel,
        grid=(2,),
        in_specs=[mant, expo, mant, expo],
        out_specs=[
            pl.BlockSpec((width, wide), lambda i: (i, 0)),
            pl.BlockSpec((width, 2 * rest), lambda i: (0, 0)),
        ],
        out_shape=[
            jax.ShapeDtypeStruct((depth, wide), jnp.bfloat16),
            jax.ShapeDtypeStruct((width, 2 * rest), jnp.bfloat16),
        ],
        compiler_params=pltpu.CompilerParams(vmem_limit_bytes=24 << 20),
        cost_estimate=pl.CostEstimate(
            flops=4 * half * depth * 64, bytes_accessed=8 * half * depth, transcendentals=0
        ),
    )(gate_mant.T, gate_expo, up_mant.T, up_expo)


def product_kernel(side_ref, rows_ref, wide_ref, rest_ref, out_ref):
    width = rows_ref.shape[-1]
    rows = jnp.transpose(rows_ref[0], (1, 2, 3, 0, 4, 5)).reshape(-1, width)
    wide, rest = wide_ref.shape[1], rest_ref.shape[1] // 2

    def dot(x, y):
        return jnp.dot(x, y, preferred_element_type=jnp.float32)

    out_ref[:, :wide] = dot(rows, wide_ref[...])
    lower = dot(rows[:, : width // 2], rest_ref[...])
    upper = dot(rows[:, width // 2 :], rest_ref[...])
    out_ref[:, wide:] = lower[:, :rest] + upper[:, rest:]


def product(side, everyone, weights):
    wide, rest = weights
    count, units = everyone.size // everyone.shape[-1] // 2, wide.shape[1] + rest.shape[1] // 2
    return pl.pallas_call(
        product_kernel,
        grid_spec=pltpu.PrefetchScalarGridSpec(
            num_scalar_prefetch=1,
            grid=(1,),
            in_specs=[
                pl.BlockSpec((1,) + everyone.shape[1:], lambda i, side: (side[0],) + (0,) * 6),
                pl.BlockSpec(wide.shape, lambda i, side: (0, 0)),
                pl.BlockSpec(rest.shape, lambda i, side: (0, 0)),
            ],
            out_specs=pl.BlockSpec((count, units), lambda i, side: (0, 0)),
        ),
        out_shape=jax.ShapeDtypeStruct((count, units), jnp.float32),
        compiler_params=pltpu.CompilerParams(vmem_limit_bytes=24 << 20),
        cost_estimate=pl.CostEstimate(
            flops=2 * count * wide.size, bytes_accessed=2 * wide.size, transcendentals=0
        ),
    )(side.reshape(1), everyone, wide, rest)


def summed_shares(everyone, weights):
    core = lax.axis_index("c")
    theirs = lax.ppermute(product(1 - core, everyone, weights), "c", [(0, 1), (1, 0)])
    pair = product(core, everyone, weights) + theirs
    parts = lax.all_to_all(pair.reshape(4, 32, -1), "yh", 0, 0)
    return jnp.sum(parts, axis=0)


def copied_kernel(block_ref, out_ref):
    out_ref[...] = jnp.broadcast_to(block_ref[...][None], out_ref.shape)


def copied(block, count):
    return pl.pallas_call(
        copied_kernel,
        out_shape=jax.ShapeDtypeStruct((count,) + block.shape, block.dtype),
        compiler_params=pltpu.CompilerParams(vmem_limit_bytes=16 << 20),
    )(block)


def squares():
    groups = []
    for outer, a, yl, b in itertools.product(range(8), range(4), range(2), range(4)):
        core = outer % 2
        zs = sorted(((2 * a + core) % 8, (2 * a + core + 1) % 8), key=lambda z: z % 2)
        xs = sorted(((2 * b + core) % 8, (2 * b + core + 1) % 8), key=lambda x: x % 2)
        groups.append([((outer * 8 + z) * 2 + yl) * 8 + x for z in zs for x in xs])
    return groups


def gathered(tok_mant, tok_expo):
    far = lax.all_to_all(scaled_copies(tok_mant, tok_expo, 32), FAR, 0, 0)
    copies = copied(far, 4)
    near = lax.all_to_all(copies, AXES, 0, 0, axis_index_groups=squares())
    return near.reshape((2, 2, 4, 2, 4) + tok_mant.shape)


def local(tok_mant, tok_expo, gate_mant, gate_expo, up_mant, up_expo):
    weights = scaled_weights(gate_mant, gate_expo, up_mant, up_expo)
    half = gate_mant.shape[1]
    everyone = gathered(tok_mant, tok_expo)
    summed = summed_shares(everyone, weights)
    return (jax.nn.silu(summed[:, :half]) * summed[:, half:]).astype(jnp.bfloat16)


def solution(mesh):
    fine = Mesh(mesh.devices.reshape(SIZES), AXES)
    placed = (
        P(INNER, OUTER),
        P(INNER, OUTER),
        P(OUTER, INNER),
        P(OUTER, INNER),
        P(OUTER, INNER),
        P(OUTER, INNER),
    )
    return jax.shard_map(
        local, mesh=fine, in_specs=placed, out_specs=P(OUTER, INNER), check_vma=False
    )
```

```python
import functools
import itertools

import jax
import jax.numpy as jnp
from jax import lax
from jax.experimental import pallas as pl
from jax.experimental.pallas import tpu as pltpu
from jax.sharding import Mesh
from jax.sharding import PartitionSpec as P

AXES = ("yh", "c", "zh", "zl", "yl", "xh", "xl")
SIZES = (4, 2, 4, 2, 2, 4, 2)
OUTER = ("yh", "c")
INNER = ("zh", "zl", "yl", "xh", "xl")
FAR = ("zh", "yl", "xh")


def copies_kernel(mant_ref, expo_ref, out_ref):
    blocks, width = expo_ref.shape[1], mant_ref.shape[1]
    group = lax.broadcasted_iota(jnp.int32, (blocks, width), 1) // (width // blocks)
    spread = (group == lax.broadcasted_iota(jnp.int32, (blocks, width), 0)).astype(jnp.bfloat16)
    factor = jnp.exp2(expo_ref[...].astype(jnp.float32)).astype(jnp.bfloat16)
    scale = jnp.dot(factor, spread, preferred_element_type=jnp.float32)
    scaled = (mant_ref[...].astype(jnp.float32) * scale).astype(jnp.bfloat16)
    out_ref[...] = jnp.broadcast_to(scaled[None], out_ref.shape)


def scaled_copies(mant, expo, count):
    return pl.pallas_call(
        copies_kernel,
        out_shape=jax.ShapeDtypeStruct((count,) + mant.shape, jnp.bfloat16),
        compiler_params=pltpu.CompilerParams(vmem_limit_bytes=56 << 20),
    )(mant, expo)


def weights_kernel(gate_ref, gate_expo_ref, up_ref, up_expo_ref, wide_ref, rest_ref):
    def scaled(mant_ref, expo_ref):
        factor = jnp.exp2(expo_ref[...].astype(jnp.float32)).astype(jnp.bfloat16)
        scale = lax.dot_general(
            factor, spread, (((0,), (0,)), ((), ())), preferred_element_type=jnp.float32
        )
        return (mant_ref[...].astype(jnp.float32) * scale).astype(jnp.bfloat16)

    blocks, width = gate_expo_ref.shape[0], gate_ref.shape[1]
    step = pl.program_id(0)
    block = (step * width + lax.broadcasted_iota(jnp.int32, (blocks, width), 1)) // 32
    spread = (block == lax.broadcasted_iota(jnp.int32, (blocks, width), 0)).astype(jnp.bfloat16)
    both = (scaled(gate_ref, gate_expo_ref), scaled(up_ref, up_expo_ref))
    turned = jnp.concatenate(both, axis=0).T
    wide = wide_ref.shape[1]
    rest = turned.shape[1] - wide
    wide_ref[...] = turned[:, :wide]
    for half in range(2):

        @pl.when(step == half)
        def _():
            rest_ref[:, half * rest : (half + 1) * rest] = turned[:, wide:]


def scaled_weights(gate_mant, gate_expo, up_mant, up_expo):
    depth, half = gate_mant.shape
    width = depth // 2
    wide = 2 * half // 128 * 128
    rest = 2 * half - wide
    mant = pl.BlockSpec((half, width), lambda i: (0, i))
    expo = pl.BlockSpec(gate_expo.shape, lambda i: (0, 0))
    return pl.pallas_call(
        weights_kernel,
        grid=(2,),
        in_specs=[mant, expo, mant, expo],
        out_specs=[
            pl.BlockSpec((width, wide), lambda i: (i, 0)),
            pl.BlockSpec((width, 2 * rest), lambda i: (0, 0)),
        ],
        out_shape=[
            jax.ShapeDtypeStruct((depth, wide), jnp.bfloat16),
            jax.ShapeDtypeStruct((width, 2 * rest), jnp.bfloat16),
        ],
        compiler_params=pltpu.CompilerParams(vmem_limit_bytes=24 << 20),
        cost_estimate=pl.CostEstimate(
            flops=4 * half * depth * 64, bytes_accessed=8 * half * depth, transcendentals=0
        ),
    )(gate_mant.T, gate_expo, up_mant.T, up_expo)


def product_kernel(side_ref, rows_ref, wide_ref, rest_ref, out_ref):
    width = rows_ref.shape[-1]
    rows = jnp.transpose(rows_ref[0], (1, 2, 3, 0, 4, 5)).reshape(-1, width)
    wide, rest = wide_ref.shape[1], rest_ref.shape[1] // 2

    def dot(x, y):
        return jnp.dot(x, y, preferred_element_type=jnp.float32)

    out_ref[:, :wide] = dot(rows, wide_ref[...])
    lower = dot(rows[:, : width // 2], rest_ref[...])
    upper = dot(rows[:, width // 2 :], rest_ref[...])
    out_ref[:, wide:] = lower[:, :rest] + upper[:, rest:]


def product(side, everyone, weights):
    wide, rest = weights
    count, units = everyone.size // everyone.shape[-1] // 2, wide.shape[1] + rest.shape[1] // 2
    return pl.pallas_call(
        product_kernel,
        grid_spec=pltpu.PrefetchScalarGridSpec(
            num_scalar_prefetch=1,
            grid=(1,),
            in_specs=[
                pl.BlockSpec((1,) + everyone.shape[1:], lambda i, side: (side[0],) + (0,) * 6),
                pl.BlockSpec(wide.shape, lambda i, side: (0, 0)),
                pl.BlockSpec(rest.shape, lambda i, side: (0, 0)),
            ],
            out_specs=pl.BlockSpec((count, units), lambda i, side: (0, 0)),
        ),
        out_shape=jax.ShapeDtypeStruct((count, units), jnp.float32),
        compiler_params=pltpu.CompilerParams(vmem_limit_bytes=24 << 20),
        cost_estimate=pl.CostEstimate(
            flops=2 * count * wide.size, bytes_accessed=2 * wide.size, transcendentals=0
        ),
    )(side.reshape(1), everyone, wide, rest)


def message_kernel(own_ref, theirs_ref, out_ref):
    units = own_ref.shape[1]
    pair = own_ref[...] + theirs_ref[...]
    is_gate = lax.broadcasted_iota(jnp.int32, pair.shape, 1) < units // 2
    size = jnp.abs(pair)

    def power(values):
        top = jnp.max(values, axis=1, keepdims=True)
        return jnp.ceil(jnp.log2(jnp.maximum(top, 2.0**-100)))

    gate_power = power(jnp.where(is_gate, size, 0.0))
    up_power = power(jnp.where(is_gate, 0.0, size))
    scale = jnp.where(is_gate, jnp.exp2(15.0 - gate_power), jnp.exp2(15.0 - up_power))
    coded = jnp.clip(jnp.round(pair * scale), -32767.0, 32767.0)
    out_ref[:, :units] = coded.astype(jnp.int32).astype(jnp.int16)
    rows, spare = out_ref.shape[0], out_ref.shape[1] - units
    first = lax.broadcasted_iota(jnp.int32, (rows, spare), 1) < spare // 2
    powers = jnp.where(first, gate_power, up_power)
    out_ref[:, units:] = powers.astype(jnp.int32).astype(jnp.int16)


def hidden_kernel(half, parts_ref, out_ref):
    parts = parts_ref[...].astype(jnp.int32).astype(jnp.float32)
    spare = (parts.shape[2] - 2 * half) // 2

    def total(first, place):
        scale = jnp.exp2(parts[:, :, place : place + 1] - 15.0)
        return jnp.sum(parts[:, :, first : first + half] * scale, axis=0)

    gate, upper = total(0, 2 * half), total(half, 2 * half + spare)
    out_ref[...] = (jax.nn.silu(gate) * upper).astype(jnp.bfloat16)


def hidden_share(everyone, weights):
    core = lax.axis_index("c")
    theirs = lax.ppermute(product(1 - core, everyone, weights), "c", [(0, 1), (1, 0)])
    own = product(core, everyone, weights)
    count, units = own.shape
    message = pl.pallas_call(
        message_kernel,
        out_shape=jax.ShapeDtypeStruct((count, units + 64), jnp.int16),
        compiler_params=pltpu.CompilerParams(vmem_limit_bytes=16 << 20),
    )(own, theirs)
    parts = lax.all_to_all(message.reshape(4, count // 4, units + 64), "yh", 0, 0)
    return pl.pallas_call(
        functools.partial(hidden_kernel, units // 2),
        out_shape=jax.ShapeDtypeStruct((count // 4, units // 2), jnp.bfloat16),
        compiler_params=pltpu.CompilerParams(vmem_limit_bytes=16 << 20),
    )(parts)


def copied_kernel(block_ref, out_ref):
    out_ref[...] = jnp.broadcast_to(block_ref[...][None], out_ref.shape)


def copied(block, count):
    return pl.pallas_call(
        copied_kernel,
        out_shape=jax.ShapeDtypeStruct((count,) + block.shape, block.dtype),
        compiler_params=pltpu.CompilerParams(vmem_limit_bytes=16 << 20),
    )(block)


def squares():
    groups = []
    for outer, a, yl, b in itertools.product(range(8), range(4), range(2), range(4)):
        core = outer % 2
        zs = sorted(((2 * a + core) % 8, (2 * a + core + 1) % 8), key=lambda z: z % 2)
        xs = sorted(((2 * b + core) % 8, (2 * b + core + 1) % 8), key=lambda x: x % 2)
        groups.append([((outer * 8 + z) * 2 + yl) * 8 + x for z in zs for x in xs])
    return groups


def gathered(tok_mant, tok_expo):
    far = lax.all_to_all(scaled_copies(tok_mant, tok_expo, 32), FAR, 0, 0)
    copies = copied(far, 4)
    near = lax.all_to_all(copies, AXES, 0, 0, axis_index_groups=squares())
    return near.reshape((2, 2, 4, 2, 4) + tok_mant.shape)


def local(tok_mant, tok_expo, gate_mant, gate_expo, up_mant, up_expo):
    weights = scaled_weights(gate_mant, gate_expo, up_mant, up_expo)
    return hidden_share(gathered(tok_mant, tok_expo), weights)


def solution(mesh):
    fine = Mesh(mesh.devices.reshape(SIZES), AXES)
    placed = (
        P(INNER, OUTER),
        P(INNER, OUTER),
        P(OUTER, INNER),
        P(OUTER, INNER),
        P(OUTER, INNER),
        P(OUTER, INNER),
    )
    return jax.shard_map(
        local, mesh=fine, in_specs=placed, out_specs=P(OUTER, INNER), check_vma=False
    )
```

```python
import functools
import itertools

import jax
import jax.numpy as jnp
from jax import lax
from jax.experimental import pallas as pl
from jax.experimental.pallas import tpu as pltpu
from jax.sharding import Mesh
from jax.sharding import PartitionSpec as P

AXES = ("yh", "c", "zh", "zl", "yl", "xh", "xl")
SIZES = (4, 2, 4, 2, 2, 4, 2)
OUTER = ("yh", "c")
INNER = ("zh", "zl", "yl", "xh", "xl")
FAR = ("zh", "yl", "xh")
KEPT = 512


def copies_kernel(mant_ref, expo_ref, out_ref):
    blocks, width = expo_ref.shape[1], mant_ref.shape[1]
    group = lax.broadcasted_iota(jnp.int32, (blocks, width), 1) // (width // blocks)
    spread = (group == lax.broadcasted_iota(jnp.int32, (blocks, width), 0)).astype(jnp.bfloat16)
    factor = jnp.exp2(expo_ref[...].astype(jnp.float32)).astype(jnp.bfloat16)
    scale = jnp.dot(factor, spread, preferred_element_type=jnp.float32)
    scaled = (mant_ref[...].astype(jnp.float32) * scale).astype(jnp.bfloat16)
    out_ref[...] = jnp.broadcast_to(scaled[None], out_ref.shape)


def scaled_copies(mant, expo, count):
    return pl.pallas_call(
        copies_kernel,
        out_shape=jax.ShapeDtypeStruct((count,) + mant.shape, jnp.bfloat16),
        compiler_params=pltpu.CompilerParams(vmem_limit_bytes=56 << 20),
    )(mant, expo)


def weights_kernel(gate_ref, gate_expo_ref, up_ref, up_expo_ref, kept_ref, wide_ref, rest_ref):
    def scaled(mant_ref, expo_ref):
        factor = jnp.exp2(expo_ref[...].astype(jnp.float32)).astype(jnp.bfloat16)
        scale = lax.dot_general(
            factor, spread, (((0,), (0,)), ((), ())), preferred_element_type=jnp.float32
        )
        return (mant_ref[...].astype(jnp.float32) * scale).astype(jnp.bfloat16)

    blocks, width = gate_expo_ref.shape[0], gate_ref.shape[1]
    step = pl.program_id(0)
    block = (step * width + lax.broadcasted_iota(jnp.int32, (blocks, width), 1)) // 32
    spread = (block == lax.broadcasted_iota(jnp.int32, (blocks, width), 0)).astype(jnp.bfloat16)
    both = (scaled(gate_ref, gate_expo_ref), scaled(up_ref, up_expo_ref))
    turned = jnp.concatenate(both, axis=0).T
    kept = kept_ref.shape[1]
    wide = kept + wide_ref.shape[1]
    rest = turned.shape[1] - wide
    kept_ref[...] = turned[:, :kept]
    wide_ref[...] = turned[:, kept:wide]
    for half in range(2):

        @pl.when(step == half)
        def _():
            rest_ref[:, half * rest : (half + 1) * rest] = turned[:, wide:]


def scaled_weights(gate_mant, gate_expo, up_mant, up_expo):
    depth, half = gate_mant.shape
    width = depth // 2
    wide = 2 * half // 128 * 128
    rest = 2 * half - wide
    mant = pl.BlockSpec((half, width), lambda i: (0, i))
    expo = pl.BlockSpec(gate_expo.shape, lambda i: (0, 0))
    return pl.pallas_call(
        weights_kernel,
        grid=(2,),
        in_specs=[mant, expo, mant, expo],
        out_specs=[
            pl.BlockSpec((width, KEPT), lambda i: (i, 0)),
            pl.BlockSpec((width, wide - KEPT), lambda i: (i, 0)),
            pl.BlockSpec((width, 2 * rest), lambda i: (0, 0)),
        ],
        out_shape=[
            jax.ShapeDtypeStruct((depth, KEPT), jnp.bfloat16),
            jax.ShapeDtypeStruct((depth, wide - KEPT), jnp.bfloat16),
            jax.ShapeDtypeStruct((width, 2 * rest), jnp.bfloat16),
        ],
        compiler_params=pltpu.CompilerParams(vmem_limit_bytes=24 << 20),
        cost_estimate=pl.CostEstimate(
            flops=4 * half * depth * 64, bytes_accessed=8 * half * depth, transcendentals=0
        ),
    )(gate_mant.T, gate_expo, up_mant.T, up_expo)


def product_kernel(side_ref, rows_ref, kept_ref, wide_ref, rest_ref, out_ref):
    width = rows_ref.shape[-1]
    rows = jnp.transpose(rows_ref[0], (1, 2, 3, 0, 4, 5)).reshape(-1, width)
    kept, rest = kept_ref.shape[1], rest_ref.shape[1] // 2
    wide = kept + wide_ref.shape[1]

    def dot(x, y):
        return jnp.dot(x, y, preferred_element_type=jnp.float32)

    out_ref[:, :kept] = dot(rows, kept_ref[...])
    out_ref[:, kept:wide] = dot(rows, wide_ref[...])
    lower = dot(rows[:, : width // 2], rest_ref[...])
    upper = dot(rows[:, width // 2 :], rest_ref[...])
    out_ref[:, wide:] = lower[:, :rest] + upper[:, rest:]


def product(side, everyone, weights):
    kept, wide, rest = weights
    units = kept.shape[1] + wide.shape[1] + rest.shape[1] // 2
    count = everyone.size // everyone.shape[-1] // 2
    return pl.pallas_call(
        product_kernel,
        grid_spec=pltpu.PrefetchScalarGridSpec(
            num_scalar_prefetch=1,
            grid=(1,),
            in_specs=[
                pl.BlockSpec((1,) + everyone.shape[1:], lambda i, side: (side[0],) + (0,) * 6),
                pl.BlockSpec(kept.shape, lambda i, side: (0, 0)),
                pl.BlockSpec(wide.shape, lambda i, side: (0, 0)),
                pl.BlockSpec(rest.shape, lambda i, side: (0, 0)),
            ],
            out_specs=pl.BlockSpec((count, units), lambda i, side: (0, 0)),
        ),
        out_shape=jax.ShapeDtypeStruct((count, units), jnp.float32),
        compiler_params=pltpu.CompilerParams(vmem_limit_bytes=24 << 20),
        cost_estimate=pl.CostEstimate(
            flops=2 * count * units * everyone.shape[-1],
            bytes_accessed=2 * units * everyone.shape[-1],
            transcendentals=0,
        ),
    )(side.reshape(1), everyone, kept, wide, rest)


def message_kernel(own_ref, theirs_ref, out_ref):
    units = own_ref.shape[1]
    pair = own_ref[...] + theirs_ref[...]
    is_gate = lax.broadcasted_iota(jnp.int32, pair.shape, 1) < units // 2
    size = jnp.abs(pair)

    def power(values):
        top = jnp.max(values, axis=1, keepdims=True)
        return jnp.ceil(jnp.log2(jnp.maximum(top, 2.0**-100)))

    gate_power = power(jnp.where(is_gate, size, 0.0))
    up_power = power(jnp.where(is_gate, 0.0, size))
    scale = jnp.where(is_gate, jnp.exp2(15.0 - gate_power), jnp.exp2(15.0 - up_power))
    coded = jnp.clip(jnp.round(pair * scale), -32767.0, 32767.0)
    out_ref[:, :units] = coded.astype(jnp.int32).astype(jnp.int16)
    rows, spare = out_ref.shape[0], out_ref.shape[1] - units
    first = lax.broadcasted_iota(jnp.int32, (rows, spare), 1) < spare // 2
    powers = jnp.where(first, gate_power, up_power)
    out_ref[:, units:] = powers.astype(jnp.int32).astype(jnp.int16)


def hidden_kernel(half, parts_ref, out_ref):
    parts = parts_ref[...].astype(jnp.int32).astype(jnp.float32)
    spare = (parts.shape[2] - 2 * half) // 2

    def total(first, place):
        scale = jnp.exp2(parts[:, :, place : place + 1] - 15.0)
        return jnp.sum(parts[:, :, first : first + half] * scale, axis=0)

    gate, upper = total(0, 2 * half), total(half, 2 * half + spare)
    out_ref[...] = (jax.nn.silu(gate) * upper).astype(jnp.bfloat16)


def hidden_share(everyone, weights):
    core = lax.axis_index("c")
    theirs = lax.ppermute(product(1 - core, everyone, weights), "c", [(0, 1), (1, 0)])
    own = product(core, everyone, weights)
    count, units = own.shape
    message = pl.pallas_call(
        message_kernel,
        out_shape=jax.ShapeDtypeStruct((count, units + 64), jnp.int16),
        compiler_params=pltpu.CompilerParams(vmem_limit_bytes=16 << 20),
    )(own, theirs)
    parts = lax.all_to_all(message.reshape(4, count // 4, units + 64), "yh", 0, 0)
    return pl.pallas_call(
        functools.partial(hidden_kernel, units // 2),
        out_shape=jax.ShapeDtypeStruct((count // 4, units // 2), jnp.bfloat16),
        compiler_params=pltpu.CompilerParams(vmem_limit_bytes=16 << 20),
    )(parts)


def copied_kernel(block_ref, out_ref):
    out_ref[...] = jnp.broadcast_to(block_ref[...][None], out_ref.shape)


def copied(block, count):
    return pl.pallas_call(
        copied_kernel,
        out_shape=jax.ShapeDtypeStruct((count,) + block.shape, block.dtype),
        compiler_params=pltpu.CompilerParams(vmem_limit_bytes=16 << 20),
    )(block)


def squares():
    groups = []
    for outer, a, yl, b in itertools.product(range(8), range(4), range(2), range(4)):
        core = outer % 2
        zs = sorted(((2 * a + core) % 8, (2 * a + core + 1) % 8), key=lambda z: z % 2)
        xs = sorted(((2 * b + core) % 8, (2 * b + core + 1) % 8), key=lambda x: x % 2)
        groups.append([((outer * 8 + z) * 2 + yl) * 8 + x for z in zs for x in xs])
    return groups


def gathered(tok_mant, tok_expo):
    far = lax.all_to_all(scaled_copies(tok_mant, tok_expo, 32), FAR, 0, 0)
    copies = copied(far, 4)
    near = lax.all_to_all(copies, AXES, 0, 0, axis_index_groups=squares())
    return near.reshape((2, 2, 4, 2, 4) + tok_mant.shape)


def local(tok_mant, tok_expo, gate_mant, gate_expo, up_mant, up_expo):
    weights = scaled_weights(gate_mant, gate_expo, up_mant, up_expo)
    return hidden_share(gathered(tok_mant, tok_expo), weights)


def solution(mesh):
    fine = Mesh(mesh.devices.reshape(SIZES), AXES)
    placed = (
        P(INNER, OUTER),
        P(INNER, OUTER),
        P(OUTER, INNER),
        P(OUTER, INNER),
        P(OUTER, INNER),
        P(OUTER, INNER),
    )
    return jax.shard_map(
        local, mesh=fine, in_specs=placed, out_specs=P(OUTER, INNER), check_vma=False
    )
```

```python
import functools
import itertools

import jax
import jax.numpy as jnp
from jax import lax
from jax.experimental import pallas as pl
from jax.experimental.pallas import tpu as pltpu
from jax.sharding import Mesh
from jax.sharding import PartitionSpec as P

AXES = ("yh", "c", "zh", "zl", "yl", "xh", "xl")
SIZES = (4, 2, 4, 2, 2, 4, 2)
OUTER = ("yh", "c")
INNER = ("zh", "zl", "yl", "xh", "xl")
FAR = ("zh", "yl", "xh")
KEPT = 512
SPARE = 16


def copies_kernel(mant_ref, expo_ref, out_ref):
    blocks, width = expo_ref.shape[1], mant_ref.shape[1]
    group = lax.broadcasted_iota(jnp.int32, (blocks, width), 1) // (width // blocks)
    spread = (group == lax.broadcasted_iota(jnp.int32, (blocks, width), 0)).astype(jnp.bfloat16)
    factor = jnp.exp2(expo_ref[...].astype(jnp.float32)).astype(jnp.bfloat16)
    scale = jnp.dot(factor, spread, preferred_element_type=jnp.float32)
    scaled = (mant_ref[...].astype(jnp.float32) * scale).astype(jnp.bfloat16)
    out_ref[...] = jnp.broadcast_to(scaled[None], out_ref.shape)


def scaled_copies(mant, expo, count):
    return pl.pallas_call(
        copies_kernel,
        out_shape=jax.ShapeDtypeStruct((count,) + mant.shape, jnp.bfloat16),
        compiler_params=pltpu.CompilerParams(vmem_limit_bytes=56 << 20),
    )(mant, expo)


def weights_kernel(gate_ref, gate_expo_ref, up_ref, up_expo_ref, kept_ref, wide_ref, rest_ref):
    def scaled(mant_ref, expo_ref):
        factor = jnp.exp2(expo_ref[...].astype(jnp.float32)).astype(jnp.bfloat16)
        scale = lax.dot_general(
            factor, spread, (((0,), (0,)), ((), ())), preferred_element_type=jnp.float32
        )
        return (mant_ref[...].astype(jnp.float32) * scale).astype(jnp.bfloat16)

    blocks, width = gate_expo_ref.shape[0], gate_ref.shape[1]
    step = pl.program_id(0)
    block = (step * width + lax.broadcasted_iota(jnp.int32, (blocks, width), 1)) // 32
    spread = (block == lax.broadcasted_iota(jnp.int32, (blocks, width), 0)).astype(jnp.bfloat16)
    both = (scaled(gate_ref, gate_expo_ref), scaled(up_ref, up_expo_ref))
    turned = jnp.concatenate(both, axis=0).T
    kept = kept_ref.shape[1]
    wide = kept + wide_ref.shape[1]
    rest = turned.shape[1] - wide
    kept_ref[...] = turned[:, :kept]
    wide_ref[...] = turned[:, kept:wide]
    for half in range(2):

        @pl.when(step == half)
        def _():
            rest_ref[:, half * rest : (half + 1) * rest] = turned[:, wide:]


def scaled_weights(gate_mant, gate_expo, up_mant, up_expo):
    depth, half = gate_mant.shape
    width = depth // 2
    wide = 2 * half // 128 * 128
    rest = 2 * half - wide
    mant = pl.BlockSpec((half, width), lambda i: (0, i))
    expo = pl.BlockSpec(gate_expo.shape, lambda i: (0, 0))
    return pl.pallas_call(
        weights_kernel,
        grid=(2,),
        in_specs=[mant, expo, mant, expo],
        out_specs=[
            pl.BlockSpec((width, KEPT), lambda i: (i, 0)),
            pl.BlockSpec((width, wide - KEPT), lambda i: (i, 0)),
            pl.BlockSpec((width, 2 * rest), lambda i: (0, 0)),
        ],
        out_shape=[
            jax.ShapeDtypeStruct((depth, KEPT), jnp.bfloat16),
            jax.ShapeDtypeStruct((SPARE * depth, wide - KEPT), jnp.bfloat16),
            jax.ShapeDtypeStruct((width, 2 * rest), jnp.bfloat16),
        ],
        compiler_params=pltpu.CompilerParams(vmem_limit_bytes=40 << 20),
        cost_estimate=pl.CostEstimate(
            flops=4 * half * depth * 64, bytes_accessed=8 * half * depth, transcendentals=0
        ),
    )(gate_mant.T, gate_expo, up_mant.T, up_expo)


def product_kernel(
    side_ref, rows_ref, kept_ref, wide_hbm, rest_ref, out_ref, wide_ref, sem
):
    fetch = pltpu.make_async_copy(wide_hbm.at[pl.ds(0, wide_ref.shape[0])], wide_ref, sem)
    fetch.start()
    width = rows_ref.shape[-1]
    rows = jnp.transpose(rows_ref[0], (1, 2, 3, 0, 4, 5)).reshape(-1, width)
    kept, rest = kept_ref.shape[1], rest_ref.shape[1] // 2
    wide = kept + wide_ref.shape[1]

    def dot(x, y):
        return jnp.dot(x, y, preferred_element_type=jnp.float32)

    out_ref[:, :kept] = dot(rows, kept_ref[...])
    lower = dot(rows[:, : width // 2], rest_ref[...])
    upper = dot(rows[:, width // 2 :], rest_ref[...])
    out_ref[:, wide:] = lower[:, :rest] + upper[:, rest:]
    fetch.wait()
    out_ref[:, kept:wide] = dot(rows, wide_ref[...])


def product(side, everyone, weights):
    kept, wide, rest = weights
    units = kept.shape[1] + wide.shape[1] + rest.shape[1] // 2
    count = everyone.size // everyone.shape[-1] // 2
    return pl.pallas_call(
        product_kernel,
        grid_spec=pltpu.PrefetchScalarGridSpec(
            num_scalar_prefetch=1,
            grid=(1,),
            in_specs=[
                pl.BlockSpec((1,) + everyone.shape[1:], lambda i, side: (side[0],) + (0,) * 6),
                pl.BlockSpec(kept.shape, lambda i, side: (0, 0)),
                pl.BlockSpec(memory_space=pl.ANY),
                pl.BlockSpec(rest.shape, lambda i, side: (0, 0)),
            ],
            out_specs=pl.BlockSpec((count, units), lambda i, side: (0, 0)),
            scratch_shapes=[
                pltpu.VMEM((kept.shape[0], wide.shape[1]), wide.dtype),
                pltpu.SemaphoreType.DMA,
            ],
        ),
        out_shape=jax.ShapeDtypeStruct((count, units), jnp.float32),
        compiler_params=pltpu.CompilerParams(vmem_limit_bytes=50 << 20),
        cost_estimate=pl.CostEstimate(
            flops=2 * count * units * everyone.shape[-1],
            bytes_accessed=2 * units * everyone.shape[-1],
            transcendentals=0,
        ),
    )(side.reshape(1), everyone, kept, wide, rest)


def message_kernel(own_ref, theirs_ref, out_ref):
    units = own_ref.shape[1]
    pair = own_ref[...] + theirs_ref[...]
    is_gate = lax.broadcasted_iota(jnp.int32, pair.shape, 1) < units // 2
    size = jnp.abs(pair)

    def power(values):
        top = jnp.max(values, axis=1, keepdims=True)
        return jnp.ceil(jnp.log2(jnp.maximum(top, 2.0**-100)))

    gate_power = power(jnp.where(is_gate, size, 0.0))
    up_power = power(jnp.where(is_gate, 0.0, size))
    scale = jnp.where(is_gate, jnp.exp2(15.0 - gate_power), jnp.exp2(15.0 - up_power))
    coded = jnp.clip(jnp.round(pair * scale), -32767.0, 32767.0)
    out_ref[:, :units] = coded.astype(jnp.int32).astype(jnp.int16)
    rows, spare = out_ref.shape[0], out_ref.shape[1] - units
    first = lax.broadcasted_iota(jnp.int32, (rows, spare), 1) < spare // 2
    powers = jnp.where(first, gate_power, up_power)
    out_ref[:, units:] = powers.astype(jnp.int32).astype(jnp.int16)


def hidden_kernel(half, parts_ref, out_ref):
    parts = parts_ref[...].astype(jnp.int32).astype(jnp.float32)
    spare = (parts.shape[2] - 2 * half) // 2

    def total(first, place):
        scale = jnp.exp2(parts[:, :, place : place + 1] - 15.0)
        return jnp.sum(parts[:, :, first : first + half] * scale, axis=0)

    gate, upper = total(0, 2 * half), total(half, 2 * half + spare)
    out_ref[...] = (jax.nn.silu(gate) * upper).astype(jnp.bfloat16)


def hidden_share(everyone, weights):
    core = lax.axis_index("c")
    theirs = lax.ppermute(product(1 - core, everyone, weights), "c", [(0, 1), (1, 0)])
    own = product(core, everyone, weights)
    count, units = own.shape
    message = pl.pallas_call(
        message_kernel,
        out_shape=jax.ShapeDtypeStruct((count, units + 64), jnp.int16),
        compiler_params=pltpu.CompilerParams(vmem_limit_bytes=16 << 20),
    )(own, theirs)
    parts = lax.all_to_all(message.reshape(4, count // 4, units + 64), "yh", 0, 0)
    return pl.pallas_call(
        functools.partial(hidden_kernel, units // 2),
        out_shape=jax.ShapeDtypeStruct((count // 4, units // 2), jnp.bfloat16),
        compiler_params=pltpu.CompilerParams(vmem_limit_bytes=16 << 20),
    )(parts)


def copied_kernel(block_ref, out_ref):
    out_ref[...] = jnp.broadcast_to(block_ref[...][None], out_ref.shape)


def copied(block, count):
    return pl.pallas_call(
        copied_kernel,
        out_shape=jax.ShapeDtypeStruct((count,) + block.shape, block.dtype),
        compiler_params=pltpu.CompilerParams(vmem_limit_bytes=16 << 20),
    )(block)


def squares():
    groups = []
    for outer, a, yl, b in itertools.product(range(8), range(4), range(2), range(4)):
        core = outer % 2
        zs = sorted(((2 * a + core) % 8, (2 * a + core + 1) % 8), key=lambda z: z % 2)
        xs = sorted(((2 * b + core) % 8, (2 * b + core + 1) % 8), key=lambda x: x % 2)
        groups.append([((outer * 8 + z) * 2 + yl) * 8 + x for z in zs for x in xs])
    return groups


def gathered(tok_mant, tok_expo):
    far = lax.all_to_all(scaled_copies(tok_mant, tok_expo, 32), FAR, 0, 0)
    copies = copied(far, 4)
    near = lax.all_to_all(copies, AXES, 0, 0, axis_index_groups=squares())
    return near.reshape((2, 2, 4, 2, 4) + tok_mant.shape)


def local(tok_mant, tok_expo, gate_mant, gate_expo, up_mant, up_expo):
    weights = scaled_weights(gate_mant, gate_expo, up_mant, up_expo)
    return hidden_share(gathered(tok_mant, tok_expo), weights)


def solution(mesh):
    fine = Mesh(mesh.devices.reshape(SIZES), AXES)
    placed = (
        P(INNER, OUTER),
        P(INNER, OUTER),
        P(OUTER, INNER),
        P(OUTER, INNER),
        P(OUTER, INNER),
        P(OUTER, INNER),
    )
    return jax.shard_map(
        local, mesh=fine, in_specs=placed, out_specs=P(OUTER, INNER), check_vma=False
    )
```
